512 devices in a mesh: expert: 64 (over z, y_lo, core), shard: 8 (over x, y_hi).
Axes of the slice: x: 4, y: 8 (y_hi: 2, y_lo: 4; y = y_hi * 4 + y_lo), z: 8, core: 2. Of those that a mesh axis runs over, the one named last changes fastest.
Arguments:
- tokens: bfloat16 [16384, 2048], P(('expert', 'shard')), may hold values from -6 to 6
- routes: int32 [16384, 8], P(('expert', 'shard')), may hold values from 0 to 63, all different within a row; in each aligned block of 32 rows (0 to 31, 32 to 63, ...) at most 8 rows name the same one
- master: float32 [64, 2, 768, 2048], P('expert', None, 'shard'), may hold values from -0.125 to 0.125
- moment1: bfloat16 [64, 2, 768, 2048], P('expert', None, 'shard'), may hold values from -1.796875 to 1.796875
- moment2: bfloat16 [64, 2, 768, 2048], P('expert', None, 'shard'), may hold values from 0.0099487305 to 1
- grads: bfloat16 [64, 2, 768, 2048], P('expert', None, 'shard'), may hold values from -6 to 6
- owner_old: int32 [64], replicated, may hold values from 0 to 63, as said below
- owner_new: int32 [64], replicated, may hold values from 0 to 63, as said below
Outputs:
- hidden: bfloat16 [64, 768, 4096], P('expert', 'shard')
The draws below stay inside these ranges and needn't reach their ends.
Inputs may be any that keep to these rules, and one draw needn't show every extreme that they name: `routes`: in the rows of one device (aligned blocks of 32 tokens) no expert is named more than 8 times, and each token names 8 different experts. `owner_old`: every owner holds exactly one expert. Every owner receives exactly one expert; owner_new[e] is owner_old[e] or the owner half the expert axis away (owner_old[e] plus or minus 64 // 2), and the two experts of such a pair trade owners. The experts of owners 0 and 32 always trade.
All inputs are finite; a program needn't handle non-finite values.
Results may differ from the reference program's by a relative error of at most 0.0058.
Values may be sent and summed in bfloat16 or wider, within the bound.
No kernel may reach another device: no remote copies, remote signals or barrier semaphores. Data moves between devices by JAX's collectives and lax.ppermute only.
A program may use at most 64 MiB of HBM per device.

```python
import math
import jax
import jax.numpy as jnp
import numpy as np
from jax import lax

D = 2048
HID = 768
TOP = 8
TOK_DEV = 32
EXPERTS = 64
CAP = 8
ROWS = 4096
TOKENS = 16384
N_EXPERT = 64
N_SHARD = 8


def owner_tables(key):
    ordering = jax.random.permutation(key, EXPERTS).astype(jnp.int32)
    halfway = EXPERTS // 2
    flipped = jax.random.randint(jax.random.fold_in(key, 11), (halfway,), 0, 2)
    flipped = flipped.at[0].set(1)
    paired = jnp.concatenate([flipped, flipped])
    moving = paired[ordering]
    renewed = jnp.where(moving == 1, (ordering + halfway) % EXPERTS, ordering)
    return (ordering, renewed.astype(jnp.int32))


def draw_owner_old(key, part):
    return owner_tables(key)[0]


def draw_owner_new(key, part):
    return owner_tables(key)[1]


def shard_levels(key, shape, cuts, least, high):
    factor_of = 1.0
    for dim, parts in cuts:
        heights = jax.random.uniform(jax.random.fold_in(jax.random.fold_in(key, 6), dim), (parts,), jnp.float32, least / len(cuts), high / len(cuts))
        factor_of = factor_of * jnp.repeat(jnp.exp(heights), shape[dim] // parts).reshape((-1,) + (1,) * (len(shape) - 1 - dim))
    return factor_of


def routed_block(key, own, number, rows, count, top, most, skew):
    sequence = jax.random.permutation(key, count)
    packed, usual = portions_of(count, rows * top, most, skew, True), portions_of(count, rows * top, most, skew, False)
    places = jnp.arange(count)

    def named(sizes, rotation):
        used = int((sizes > 0).sum())
        fixed = max(1, used // 4)
        moved = fixed + (places - fixed + rotation * (used - fixed)) % max(1, count - fixed)
        return jnp.zeros((count,), jnp.int32).at[sequence[jnp.where(places < fixed, places, moved)]].set(jnp.asarray(sizes, jnp.int32))

    sizes = jnp.where(number % 4 == 0, named(packed, number // 4), named(usual, number - number // 4 - 1))
    mixed = jax.random.permutation(jax.random.fold_in(own, 3), count)
    source_of, sink = mixed[0:count // 2 * 2:2], mixed[1:count // 2 * 2:2]
    room = jnp.minimum(sizes[source_of] - 1, most - sizes[sink]) // 2
    room = jnp.where((source_of == sequence[0]) | (sink == sequence[0]) | (sizes[sink] == 0), 0, jnp.maximum(room, 0))
    moved = jax.random.randint(jax.random.fold_in(own, 4), (count // 2,), 0, 1 << 20) % (room + 1)
    sizes = sizes.at[source_of].add(-moved).at[sink].add(moved)
    labels = jnp.searchsorted(jnp.cumsum(sizes), jnp.arange(rows * top), side="right").astype(jnp.int32)
    table = labels.reshape(top, rows).T
    table = table[jax.random.permutation(jax.random.fold_in(own, 1), rows)]
    rotation = jax.random.randint(jax.random.fold_in(own, 2), (rows, 1), 0, top)
    return jnp.take_along_axis(table, (jnp.arange(top)[None, :] + rotation) % top, axis=1)


def portions_of(amount, total, limit, lean, full):
    weights = [(1 << 20) // math.isqrt(grade ** lean) + 1 for grade in range(1, amount + 1)]
    largest = limit if full else min(limit, max(-(-total // amount), total * weights[0] // sum(weights)))
    least = 1 if total - largest >= amount - 1 else 0
    given, spare = [largest] + [least] * (amount - 1), total - largest - least * (amount - 1)
    while spare > 0:
        candidates = [i for i in range(1, amount) if given[i] < largest] or [i for i in range(1, amount) if given[i] < limit]
        pool, left = sum([weights[i] for i in candidates]), spare
        for i in candidates:
            more = min(limit - given[i], max(1, left * weights[i] // pool), spare)
            given[i] = given[i] + more
            spare = spare - more
    return np.array(given)


def scatter_about(key, dims, spread, most, cuts=(), kind=jnp.bfloat16):
    values = spread * jax.random.normal(key, dims, jnp.float32)
    if cuts:
        values = values * shard_levels(key, dims, cuts, -0.22, 0.18)
    return jnp.clip(values, -most, most).astype(kind)


def setup_inputs(seed: int = 0) -> dict:
    seeds = jax.random.split(jax.random.key(seed), 9)
    tokens = scatter_about(seeds[0], (TOKENS, D), 1.0, 6.0, ((0, 512),))
    routes_keys = jax.random.split(jax.random.fold_in(seeds[1], 1), TOKENS // TOK_DEV)
    routes_turns = jax.random.permutation(jax.random.fold_in(seeds[1], 3), TOKENS // TOK_DEV)
    routes = jax.vmap(lambda own, number: routed_block(jax.random.fold_in(seeds[1], 2), own, number, TOK_DEV, EXPERTS, TOP, CAP, 2))(routes_keys, routes_turns).reshape((TOKENS, TOP))
    master = scatter_about(seeds[2], (EXPERTS, 2, HID, D), D ** -0.5, 0.125, ((0, 64), (2, 8)), jnp.float32)
    moment1 = scatter_about(seeds[3], (EXPERTS, 2, HID, D), 0.3, 1.796875, ((0, 64), (2, 8)))
    moment2 = jnp.clip(jnp.exp(math.log(1.0) - 4.61031033 * jax.random.uniform(seeds[4], (EXPERTS, 2, HID, D), jnp.float32) ** shard_levels(seeds[4], (EXPERTS, 2, HID, D), ((0, 64), (2, 8)), -0.2, 0.2)), 0.0099487305, 1.0).astype(jnp.bfloat16)
    grads = scatter_about(seeds[5], (EXPERTS, 2, HID, D), 1.0, 6.0, ((0, 64), (2, 8)))
    owner_old = draw_owner_old(jax.random.fold_in(seeds[8], 71), 0)
    owner_new = draw_owner_new(jax.random.fold_in(seeds[8], 71), 0)
    return dict(tokens=tokens, routes=routes, master=master, moment1=moment1, moment2=moment2, grads=grads, owner_old=owner_old, owner_new=owner_new)


learn_rate = 0.003

def adam_update(master, moment1, moment2, grads):
    gradient = grads.astype(jnp.float32)
    first = 0.9 * moment1.astype(jnp.float32) + 0.1 * gradient
    second = 0.95 * moment2.astype(jnp.float32) + 0.05 * gradient * gradient
    stepped = master - learn_rate * (first / (1.0 - 0.9 ** 3)) / (jnp.sqrt(second / (1.0 - 0.95 ** 3)) + 1e-08)
    return stepped.astype(jnp.bfloat16)

def reference(tokens, routes, master, moment1, moment2, grads, owner_old, owner_new):
    blocks = N_EXPERT * N_SHARD
    source = jnp.zeros((EXPERTS,), jnp.int32).at[owner_new].set(owner_old)
    flat = routes.reshape(blocks, TOK_DEV * TOP)
    onehot = (flat[:, :, None] == jnp.arange(EXPERTS, dtype=jnp.int32)[None, None, :]).astype(jnp.int32)
    ranking = lax.optimization_barrier(jnp.sum((jnp.cumsum(onehot, axis=1) - onehot) * onehot, axis=2)).astype(jnp.int32)
    block_ids = jnp.arange(blocks, dtype=jnp.int32)[:, None]
    position = block_ids * CAP + ranking
    token_index = block_ids * TOK_DEV + (jnp.arange(TOK_DEV * TOP, dtype=jnp.int32) // TOP)[None, :]
    destination = owner_new[flat]
    slot_token = jnp.full((EXPERTS, ROWS), -1, jnp.int32).at[destination, position].set(token_index)

    def owner_hidden(items):
        anchor, slot_row = items
        weights = adam_update(master[anchor], moment1[anchor], moment2[anchor], grads[anchor])
        valid = slot_row >= 0
        picked = tokens[jnp.maximum(slot_row, 0)]
        filled = jnp.where(valid[:, None], picked, jnp.zeros((), jnp.bfloat16))
        gate = jnp.dot(weights[0], filled.T, preferred_element_type=jnp.float32)
        upward = jnp.dot(weights[1], filled.T, preferred_element_type=jnp.float32)
        return (jax.nn.silu(gate) * upward).astype(jnp.bfloat16)
    return lax.map(owner_hidden, (source, slot_token))
```

```python
import jax
import jax.numpy as jnp
from jax import lax
from jax.sharding import Mesh, PartitionSpec as P

learn_rate = 0.003
EXPERT = ("z", "y", "core")
SHARD = ("x", "w")
CHUNKS = 2
X_GATHER = "permute"


def rotate(block, axis, step):
    count = lax.axis_size(axis)
    return lax.ppermute(block, axis, [(i, (i + step) % count) for i in range(count)])


def adam_update(master, moment1, moment2, grads):
    gradient = grads.astype(jnp.float32)
    first = 0.9 * moment1.astype(jnp.float32) + 0.1 * gradient
    second = 0.95 * moment2.astype(jnp.float32) + 0.05 * gradient * gradient
    stepped = master - learn_rate * (first / (1.0 - 0.9**3)) / (
        jnp.sqrt(second / (1.0 - 0.95**3)) + 1e-08
    )
    return stepped.astype(jnp.bfloat16)


def slot_rows_to_send(tokens, routes, expert_of):
    named = jnp.any(routes[:, None, :] == expert_of[None, :, None], axis=2)
    hit = named.astype(jnp.int32)
    count = tokens.shape[0]
    earlier = jnp.arange(count)[:, None] > jnp.arange(count)[None, :]
    rank = jnp.sum(jnp.where(earlier[:, :, None], hit[None], 0), axis=1)
    capacity = 8
    pick = named.T[:, None, :] & (
        rank.T[:, None, :] == jnp.arange(capacity, dtype=jnp.int32)[None, :, None]
    )
    return jnp.einsum(
        "oct,td->ocd", pick.astype(jnp.bfloat16), tokens, preferred_element_type=jnp.float32
    ).astype(jnp.bfloat16)


def on_device(tokens, routes, master, moment1, moment2, grads, owner_old, owner_new):
    owners = lax.axis_size(EXPERT)
    myself = lax.axis_index(EXPERT)
    mine_w = lax.axis_index("w")
    mine_x = lax.axis_index("x")
    width = tokens.shape[1]
    units = master.shape[2]
    part = units // CHUNKS
    everyone = jnp.arange(owners, dtype=jnp.int32)
    held = owner_new[None, :] == everyone[:, None]
    expert_of = jnp.sum(jnp.where(held, everyone[None, :], 0), axis=1)
    source = jnp.sum(jnp.where(held[myself], owner_old, 0))
    moving = source != myself

    arrays = [a[0] for a in (master, moment1, moment2, grads)]
    gathered = []
    for j in range(CHUNKS):
        stepped = adam_update(*(a[:, j * part : (j + 1) * part] for a in arrays))
        partner = rotate(stepped, "z", 4)
        own = jnp.where(moving, partner, stepped)
        other = rotate(own, "w", 1)
        pair = jnp.where(mine_w == 0, jnp.stack([own, other]), jnp.stack([other, own]))
        if X_GATHER == "sc":
            gathered.append(lax.all_gather(pair, "x", axis=0, tiled=False))
        else:
            right = rotate(pair, "x", 1)
            left = rotate(pair, "x", -1)
            far0 = rotate(right[0], "x", 1)
            far1 = rotate(left[1], "x", -1)
            far = jnp.stack([far0, far1])
            gathered.append((pair, left, far, right))

    outgoing = slot_rows_to_send(tokens, routes, expert_of)
    arrived = lax.all_to_all(outgoing, EXPERT, split_axis=0, concat_axis=0, tiled=True)
    slot_rows = arrived.reshape(owners * 8, width)

    outs = []
    for j in range(CHUNKS):
        if X_GATHER == "sc":
            blocks = gathered[j]
        else:
            rel = jnp.stack(gathered[j])
            blocks = rel[(jnp.arange(4) - mine_x) % 4]
        both = jnp.einsum(
            "xwgud,rd->gxwur", blocks, slot_rows, preferred_element_type=jnp.float32
        )
        every = (jax.nn.silu(both[0]) * both[1]).astype(jnp.bfloat16)
        every = every.reshape(8, part, owners * 8)
        back = lax.all_to_all(every, SHARD, split_axis=0, concat_axis=0, tiled=True)
        back = back.reshape(8, part, owners, 8).transpose(1, 2, 0, 3)
        outs.append(back.reshape(part, owners * 64))
    return jnp.concatenate(outs, axis=0)[None]


def solution(mesh):
    grid = Mesh(mesh.devices.reshape(8, 4, 2, 4, 2), EXPERT + SHARD)
    rows = P(EXPERT + SHARD, None)
    units = P(EXPERT, None, SHARD, None)
    return jax.shard_map(
        on_device,
        mesh=grid,
        in_specs=(rows, rows, units, units, units, units, P(), P()),
        out_specs=P(EXPERT, SHARD, None),
        check_vma=False,
    )
```

```python
import jax
import jax.numpy as jnp
from jax import lax
from jax.sharding import Mesh, PartitionSpec as P

learn_rate = 0.003
EXPERT = ("z", "y", "core")
SHARD = ("x", "w")
CUT = 32
SEND = 'x1o1'
TIE_OWN1 = True
SPLIT_ADAM = False
TAIL = 1
CAP = 8


def rotate(block, axis, step):
    count = lax.axis_size(axis)
    return lax.ppermute(block, axis, [(i, (i + step) % count) for i in range(count)])


def after(value, *others):
    return lax.optimization_barrier((value, *others))[0]


def adam_update(master, moment1, moment2, grads):
    gradient = grads.astype(jnp.float32)
    first = 0.9 * moment1.astype(jnp.float32) + 0.1 * gradient
    second = 0.95 * moment2.astype(jnp.float32) + 0.05 * gradient * gradient
    stepped = master - learn_rate * (first / (1.0 - 0.9**3)) / (
        jnp.sqrt(second / (1.0 - 0.95**3)) + 1e-08
    )
    return stepped.astype(jnp.bfloat16)


def slot_rows(tokens, routes, experts):
    blocks, count, width = tokens.shape
    hit = jnp.any(routes[:, None, :, :] == experts[None, :, None, None], axis=3)
    order = jnp.arange(count)
    earlier = order[:, None] > order[None, :]
    rank = jnp.sum(jnp.where(earlier & hit[:, :, None, :], 1, 0), axis=3)
    pick = hit[:, :, None, :] & (rank[:, :, None, :] == jnp.arange(CAP)[:, None])
    rows = jnp.einsum(
        "bect,btd->becd", pick.astype(jnp.bfloat16), tokens, preferred_element_type=jnp.float32
    )
    return rows.astype(jnp.bfloat16).transpose(1, 0, 2, 3)


def over_x(block):
    return [block, rotate(block, "x", -1), rotate(block, "x", 2), rotate(block, "x", 1)]


def on_device(tokens, routes, master, moment1, moment2, grads, owner_old, owner_new):
    owners = lax.axis_size(EXPERT)
    myself = lax.axis_index(EXPERT)
    mine_w = lax.axis_index("w")
    mine_x = lax.axis_index("x")
    width = tokens.shape[1]
    everyone = jnp.arange(owners, dtype=jnp.int32)
    held = owner_new[None, :] == everyone[:, None]
    expert_of = jnp.sum(jnp.where(held, everyone[None, :], 0), axis=1)
    moving = jnp.sum(jnp.where(held[myself], owner_old, 0)) != myself

    arrays = [a[0] for a in (master, moment1, moment2, grads)]
    step1 = adam_update(*(a[:, :CUT] for a in arrays))
    step2 = adam_update(*(a[:, CUT:] for a in arrays))
    if SPLIT_ADAM:
        step1, *rest = lax.optimization_barrier((step1, *(a[:, CUT:] for a in arrays)))
        step2 = adam_update(*rest)
    own1 = jnp.where(moving, rotate(step1, "z", 4), step1)
    own2 = jnp.where(moving, rotate(step2, "z", 4), step2)

    wide = jnp.concatenate(
        [tokens, jnp.pad(routes, ((0, 0), (0, 120))).astype(jnp.bfloat16)], axis=1
    )
    wide = lax.all_gather(after(wide, step2), "y", axis=0, tiled=False)
    if TIE_OWN1:
        own1 = after(own1, wide)
    named = wide[:, :, width : width + routes.shape[1]].astype(jnp.int32)
    here = expert_of.reshape(8, 4, 2)[:, lax.axis_index("y")].reshape(16)
    outgoing = slot_rows(wide[:, :, :width], named, here)

    other1 = rotate(own1, "w", 1)
    first = over_x(own1)
    if SEND == "own1":
        outgoing = after(outgoing, own1)
    elif SEND == "own2":
        outgoing = after(outgoing, own2)
    elif SEND == "first":
        outgoing = after(outgoing, own2, *first[1:])
    elif SEND == "other1":
        outgoing = after(outgoing, own2, other1)
    other2 = rotate(own2, "w", 1)
    if SEND == "x1o1":
        outgoing = after(outgoing, own2, other1, *first[1:])
    elif SEND == "x1o1o2":
        outgoing = after(outgoing, own2, other1, other2, *first[1:])
    elif SEND == "o1o2":
        outgoing = after(outgoing, own2, other1, other2)
    arrived = lax.all_to_all(outgoing, ("z", "core"), split_axis=0, concat_axis=0, tiled=True)
    slots = arrived.reshape(owners * CAP, width)

    second = over_x(jnp.concatenate([other1, own2], axis=1))
    third = over_x(other2)

    def hidden_of(blocks):
        blocks = jnp.stack(blocks)
        both = jnp.einsum("xgud,rd->gxur", blocks, slots, preferred_element_type=jnp.float32)
        return (jax.nn.silu(both[0]) * both[1]).astype(jnp.bfloat16)

    placed = (jnp.arange(4) - mine_x) % 4

    def sent_back(own, other):
        every = jnp.where(
            mine_w == 0, jnp.stack([own, other], axis=1), jnp.stack([other, own], axis=1)
        )[placed]
        count = every.shape[2]
        every = every.reshape(8, count, owners * CAP)
        back = lax.all_to_all(every, SHARD, split_axis=0, concat_axis=0, tiled=True)
        back = back.reshape(8, count, 8, 2, 4, CAP).transpose(1, 2, 4, 3, 0, 5)
        return back.reshape(count, owners * 8 * CAP)

    hidden_first, hidden_second = hidden_of(first), hidden_of(second)
    if TAIL == 2:
        out1 = sent_back(hidden_first, hidden_second[:, :CUT])
        out2 = sent_back(hidden_second[:, CUT:], hidden_of(third))
        return jnp.concatenate([out1, out2], axis=0)[None]
    own = jnp.concatenate([hidden_first, hidden_second[:, CUT:]], axis=1)
    other = jnp.concatenate([hidden_second[:, :CUT], hidden_of(third)], axis=1)
    return sent_back(own, other)[None]


def solution(mesh):
    grid = Mesh(mesh.devices.reshape(8, 4, 2, 4, 2), EXPERT + SHARD)
    rows = P(EXPERT + SHARD, None)
    units = P(EXPERT, None, SHARD, None)
    return jax.shard_map(
        on_device,
        mesh=grid,
        in_specs=(rows, rows, units, units, units, units, P(), P()),
        out_specs=P(EXPERT, SHARD, None),
        check_vma=False,
    )
```

```python
import jax
import jax.numpy as jnp
from jax import lax
from jax.sharding import Mesh, PartitionSpec as P

learn_rate = 0.003
EXPERT = ("z", "y", "core")
SHARD = ("x", "w")
CUT = 32
FAR_AFTER = (1, 3)
Y_WAY = "gather"
SEND = 'x1o1+'
TIE_OWN1 = True
TAIL = 2
CAP = 8


def rotate(block, axis, step):
    count = lax.axis_size(axis)
    return lax.ppermute(block, axis, [(i, (i + step) % count) for i in range(count)])


def after(value, *others):
    return lax.optimization_barrier((value, *others))[0]


def adam_update(master, moment1, moment2, grads):
    gradient = grads.astype(jnp.float32)
    first = 0.9 * moment1.astype(jnp.float32) + 0.1 * gradient
    second = 0.95 * moment2.astype(jnp.float32) + 0.05 * gradient * gradient
    stepped = master - learn_rate * (first / (1.0 - 0.9**3)) / (
        jnp.sqrt(second / (1.0 - 0.95**3)) + 1e-08
    )
    return stepped.astype(jnp.bfloat16)


def slot_rows(tokens, routes, experts):
    blocks, count, width = tokens.shape
    routes = routes.reshape(blocks * count, -1)
    hit = jnp.any(routes[None] == experts[:, None, None], axis=2)
    place = jnp.arange(blocks * count)
    block = place // count
    earlier = (place[:, None] > place[None, :]) & (block[:, None] == block[None, :])
    rank = jnp.sum(jnp.where(earlier[None] & hit[:, None, :], 1, 0), axis=2)
    slot = jnp.where(hit, block * CAP + rank, -1)
    pick = slot[:, None, :] == jnp.arange(blocks * CAP)[None, :, None]
    pick = pick.astype(jnp.bfloat16).reshape(-1, blocks * count)
    rows = jnp.dot(pick, tokens.reshape(-1, width), preferred_element_type=jnp.float32)
    return rows.astype(jnp.bfloat16).reshape(-1, blocks, CAP, width)


def over_x(block, *others):
    far = after(block, *others) if others else block
    return [block, rotate(block, "x", -1), rotate(far, "x", 2), rotate(block, "x", 1)]


def on_device(tokens, routes, master, moment1, moment2, grads, owner_old, owner_new):
    owners = lax.axis_size(EXPERT)
    myself = lax.axis_index(EXPERT)
    mine_w = lax.axis_index("w")
    mine_x = lax.axis_index("x")
    width = tokens.shape[1]
    everyone = jnp.arange(owners, dtype=jnp.int32)
    held = owner_new[None, :] == everyone[:, None]
    expert_of = jnp.sum(jnp.where(held, everyone[None, :], 0), axis=1)
    moving = jnp.sum(jnp.where(held[myself], owner_old, 0)) != myself

    arrays = [a[0] for a in (master, moment1, moment2, grads)]
    step1 = adam_update(*(a[:, :CUT] for a in arrays))
    step2 = adam_update(*(a[:, CUT:] for a in arrays))
    own1 = jnp.where(moving, rotate(step1, "z", 4), step1)
    own2 = jnp.where(moving, rotate(step2, "z", 4), step2)

    wide = jnp.concatenate(
        [tokens, jnp.pad(routes, ((0, 0), (0, 120))).astype(jnp.bfloat16)], axis=1
    )
    wide = after(wide, step2)
    if Y_WAY == "gather":
        wide = lax.all_gather(wide, "y", axis=0, tiled=False)
    else:
        wide = jnp.broadcast_to(wide[None], (4, *wide.shape))
        wide = lax.all_to_all(wide, "y", split_axis=0, concat_axis=0, tiled=True)
    if TIE_OWN1:
        own1 = after(own1, wide)
    named = wide[:, :, width : width + routes.shape[1]].astype(jnp.int32)
    here = expert_of.reshape(8, 4, 2)[:, lax.axis_index("y")].reshape(16)
    outgoing = slot_rows(wide[:, :, :width], named, here)

    other1 = rotate(own1, "w", 1)
    first = over_x(own1)
    both = jnp.concatenate([other1, own2], axis=1)
    if SEND == "own1":
        outgoing = after(outgoing, own1)
    elif SEND == "own2":
        outgoing = after(outgoing, own2)
    elif SEND == "first":
        outgoing = after(outgoing, own2, *first[1:])
    elif SEND == "other1":
        outgoing = after(outgoing, own2, other1)
    other2 = rotate(own2, "w", 1)
    if SEND == "x1o1":
        outgoing = after(outgoing, own2, other1, *first[1:])
    elif SEND == "x1o1+":
        outgoing, both, *_ = lax.optimization_barrier((outgoing, both, *first[1:]))
    elif SEND == "x1o1o2":
        outgoing = after(outgoing, own2, other1, other2, *first[1:])
    elif SEND == "o1o2":
        outgoing = after(outgoing, own2, other1, other2)
    arrived = lax.all_to_all(outgoing, ("z", "core"), split_axis=0, concat_axis=0, tiled=True)
    slots = arrived.reshape(owners * CAP, width)

    second = over_x(both)
    third = over_x(other2, *[second[i] for i in FAR_AFTER])

    def hidden_of(blocks):
        blocks = jnp.stack(blocks)
        both = jnp.einsum("xgud,rd->gxur", blocks, slots, preferred_element_type=jnp.float32)
        return (jax.nn.silu(both[0]) * both[1]).astype(jnp.bfloat16)


    def sent_back(own, other):
        every = jnp.where(
            mine_w == 0, jnp.stack([own, other], axis=1), jnp.stack([other, own], axis=1)
        )
        every = lax.dynamic_slice_in_dim(jnp.concatenate([every, every]), (4 - mine_x) % 4, 4)
        count = every.shape[2]
        every = every.reshape(8, count, owners * CAP)
        back = lax.all_to_all(every, SHARD, split_axis=0, concat_axis=0, tiled=True)
        back = back.reshape(8, count, 8, 2, 4, CAP).transpose(1, 2, 4, 3, 0, 5)
        return back.reshape(count, owners * 8 * CAP)

    hidden_first, hidden_second = hidden_of(first), hidden_of(second)
    if TAIL == 2:
        out1 = sent_back(hidden_first, hidden_second[:, :CUT])
        out2 = sent_back(hidden_second[:, CUT:], hidden_of(third))
        return jnp.concatenate([out1, out2], axis=0)[None]
    own = jnp.concatenate([hidden_first, hidden_second[:, CUT:]], axis=1)
    other = jnp.concatenate([hidden_second[:, :CUT], hidden_of(third)], axis=1)
    return sent_back(own, other)[None]


def solution(mesh):
    grid = Mesh(mesh.devices.reshape(8, 4, 2, 4, 2), EXPERT + SHARD)
    rows = P(EXPERT + SHARD, None)
    units = P(EXPERT, None, SHARD, None)
    return jax.shard_map(
        on_device,
        mesh=grid,
        in_specs=(rows, rows, units, units, units, units, P(), P()),
        out_specs=P(EXPERT, SHARD, None),
        check_vma=False,
    )
```

```python
import jax
import jax.numpy as jnp
from jax import lax
from jax.sharding import Mesh, PartitionSpec as P

learn_rate = 0.003
EXPERT = ("z", "y", "core")
SHARD = ("x", "w")
CUT = 32
FAR_AFTER = (1, 2, 3)
Y_WAY = "gather"
SEND = 'x1o1+'
TIE_OWN1 = True
TAIL = 2
CAP = 8


def rotate(block, axis, step):
    count = lax.axis_size(axis)
    return lax.ppermute(block, axis, [(i, (i + step) % count) for i in range(count)])


def after(value, *others):
    return lax.optimization_barrier((value, *others))[0]


def adam_update(master, moment1, moment2, grads):
    gradient = grads.astype(jnp.float32)
    first = 0.9 * moment1.astype(jnp.float32) + 0.1 * gradient
    second = 0.95 * moment2.astype(jnp.float32) + 0.05 * gradient * gradient
    stepped = master - learn_rate * (first / (1.0 - 0.9**3)) / (
        jnp.sqrt(second / (1.0 - 0.95**3)) + 1e-08
    )
    return stepped.astype(jnp.bfloat16)


def slot_rows(tokens, routes, experts):
    blocks, count, width = tokens.shape
    routes = routes.reshape(blocks * count, -1)
    hit = jnp.any(routes[None] == experts[:, None, None], axis=2)
    place = jnp.arange(blocks * count)
    block = place // count
    earlier = (place[:, None] > place[None, :]) & (block[:, None] == block[None, :])
    rank = jnp.sum(jnp.where(earlier[None] & hit[:, None, :], 1, 0), axis=2)
    slot = jnp.where(hit, block * CAP + rank, -1)
    pick = slot[:, None, :] == jnp.arange(blocks * CAP)[None, :, None]
    pick = pick.astype(jnp.bfloat16).reshape(-1, blocks * count)
    rows = jnp.dot(pick, tokens.reshape(-1, width), preferred_element_type=jnp.float32)
    return rows.astype(jnp.bfloat16).reshape(-1, blocks, CAP, width)


def over_x(block, *others):
    far = after(block, *others) if others else block
    return [block, rotate(block, "x", -1), rotate(far, "x", 2), rotate(block, "x", 1)]


def on_device(tokens, routes, master, moment1, moment2, grads, owner_old, owner_new):
    owners = lax.axis_size(EXPERT)
    myself = lax.axis_index(EXPERT)
    mine_w = lax.axis_index("w")
    mine_x = lax.axis_index("x")
    width = tokens.shape[1]
    everyone = jnp.arange(owners, dtype=jnp.int32)
    held = owner_new[None, :] == everyone[:, None]
    expert_of = jnp.sum(jnp.where(held, everyone[None, :], 0), axis=1)
    moving = jnp.sum(jnp.where(held[myself], owner_old, 0)) != myself

    arrays = [a[0] for a in (master, moment1, moment2, grads)]
    step1 = adam_update(*(a[:, :CUT] for a in arrays))
    step2 = adam_update(*(a[:, CUT:] for a in arrays))
    own1 = jnp.where(moving, rotate(step1, "z", 4), step1)
    own2 = jnp.where(moving, rotate(step2, "z", 4), step2)

    wide = jnp.concatenate(
        [tokens, jnp.pad(routes, ((0, 0), (0, 120))).astype(jnp.bfloat16)], axis=1
    )
    wide = after(wide, step2)
    if Y_WAY == "gather":
        wide = lax.all_gather(wide, "y", axis=0, tiled=False)
    else:
        wide = jnp.broadcast_to(wide[None], (4, *wide.shape))
        wide = lax.all_to_all(wide, "y", split_axis=0, concat_axis=0, tiled=True)
    if TIE_OWN1:
        own1 = after(own1, wide)
    other1 = rotate(own1, "w", 1)
    wide = after(wide, other1)
    named = wide[:, :, width : width + routes.shape[1]].astype(jnp.int32)
    here = expert_of.reshape(8, 4, 2)[:, lax.axis_index("y")].reshape(16)
    outgoing = slot_rows(wide[:, :, :width], named, here)

    first = over_x(own1)
    both = jnp.concatenate([other1, own2], axis=1)
    if SEND == "own1":
        outgoing = after(outgoing, own1)
    elif SEND == "own2":
        outgoing = after(outgoing, own2)
    elif SEND == "first":
        outgoing = after(outgoing, own2, *first[1:])
    elif SEND == "other1":
        outgoing = after(outgoing, own2, other1)
    other2 = rotate(own2, "w", 1)
    if SEND == "x1o1":
        outgoing = after(outgoing, own2, other1, *first[1:])
    elif SEND == "x1o1+":
        outgoing, both, *_ = lax.optimization_barrier((outgoing, both, *first[1:]))
    elif SEND == "x1o1o2":
        outgoing = after(outgoing, own2, other1, other2, *first[1:])
    elif SEND == "o1o2":
        outgoing = after(outgoing, own2, other1, other2)
    arrived = lax.all_to_all(outgoing, ("z", "core"), split_axis=0, concat_axis=0, tiled=True)
    slots = arrived.reshape(owners * CAP, width)

    second = over_x(both)
    third = over_x(other2, *[second[i] for i in FAR_AFTER])

    def hidden_of(blocks):
        blocks = jnp.stack(blocks)
        both = jnp.einsum("xgud,rd->gxur", blocks, slots, preferred_element_type=jnp.float32)
        return (jax.nn.silu(both[0]) * both[1]).astype(jnp.bfloat16)


    def sent_back(own, other):
        every = jnp.where(
            mine_w == 0, jnp.stack([own, other], axis=1), jnp.stack([other, own], axis=1)
        )
        every = lax.dynamic_slice_in_dim(jnp.concatenate([every, every]), (4 - mine_x) % 4, 4)
        count = every.shape[2]
        every = every.reshape(8, count, owners * CAP)
        back = lax.all_to_all(every, SHARD, split_axis=0, concat_axis=0, tiled=True)
        back = back.reshape(8, count, 8, 2, 4, CAP).transpose(1, 2, 4, 3, 0, 5)
        return back.reshape(count, owners * 8 * CAP)

    hidden_first, hidden_second = hidden_of(first), hidden_of(second)
    if TAIL == 2:
        out1 = sent_back(hidden_first, hidden_second[:, :CUT])
        out2 = sent_back(hidden_second[:, CUT:], hidden_of(third))
        return jnp.concatenate([out1, out2], axis=0)[None]
    own = jnp.concatenate([hidden_first, hidden_second[:, CUT:]], axis=1)
    other = jnp.concatenate([hidden_second[:, :CUT], hidden_of(third)], axis=1)
    return sent_back(own, other)[None]


def solution(mesh):
    grid = Mesh(mesh.devices.reshape(8, 4, 2, 4, 2), EXPERT + SHARD)
    rows = P(EXPERT + SHARD, None)
    units = P(EXPERT, None, SHARD, None)
    return jax.shard_map(
        on_device,
        mesh=grid,
        in_specs=(rows, rows, units, units, units, units, P(), P()),
        out_specs=P(EXPERT, SHARD, None),
        check_vma=False,
    )
```

```python
import jax
import jax.numpy as jnp
from jax import lax
from jax.sharding import Mesh, PartitionSpec as P

learn_rate = 0.003
EXPERT = ("z", "y", "core")
SHARD = ("x", "w")
CUT = 32
FAR_AFTER = (1, 2, 3)
Y_WAY = "gather"
SEND = 'x1o1+'
TIE_OWN1 = True
TAIL = 2
CAP = 8


def rotate(block, axis, step):
    count = lax.axis_size(axis)
    return lax.ppermute(block, axis, [(i, (i + step) % count) for i in range(count)])


def after(value, *others):
    return lax.optimization_barrier((value, *others))[0]


def adam_update(master, moment1, moment2, grads):
    gradient = grads.astype(jnp.float32)
    first = 0.9 * moment1.astype(jnp.float32) + 0.1 * gradient
    second = 0.95 * moment2.astype(jnp.float32) + 0.05 * gradient * gradient
    stepped = master - learn_rate * (first / (1.0 - 0.9**3)) / (
        jnp.sqrt(second / (1.0 - 0.95**3)) + 1e-08
    )
    return stepped.astype(jnp.bfloat16)


def slot_rows(tokens, routes, experts):
    blocks, count, width = tokens.shape
    routes = routes.reshape(blocks * count, -1)
    hit = jnp.any(routes[None] == experts[:, None, None], axis=2)
    place = jnp.arange(blocks * count)
    block = place // count
    earlier = (place[:, None] > place[None, :]) & (block[:, None] == block[None, :])
    rank = jnp.sum(jnp.where(earlier[None] & hit[:, None, :], 1, 0), axis=2)
    slot = jnp.where(hit, block * CAP + rank, -1)
    pick = slot[:, None, :] == jnp.arange(blocks * CAP)[None, :, None]
    pick = pick.astype(jnp.bfloat16).reshape(-1, blocks * count)
    rows = jnp.dot(pick, tokens.reshape(-1, width), preferred_element_type=jnp.float32)
    return rows.astype(jnp.bfloat16).reshape(-1, blocks, CAP, width)


def over_x(block, *others):
    far = after(block, *others) if others else block
    return [block, rotate(block, "x", -1), rotate(far, "x", 2), rotate(block, "x", 1)]


def on_device(tokens, routes, master, moment1, moment2, grads, owner_old, owner_new):
    owners = lax.axis_size(EXPERT)
    myself = lax.axis_index(EXPERT)
    mine_w = lax.axis_index("w")
    mine_x = lax.axis_index("x")
    width = tokens.shape[1]
    everyone = jnp.arange(owners, dtype=jnp.int32)
    held = owner_new[None, :] == everyone[:, None]
    expert_of = jnp.sum(jnp.where(held, everyone[None, :], 0), axis=1)
    moving = jnp.sum(jnp.where(held[myself], owner_old, 0)) != myself

    arrays = [a[0] for a in (master, moment1, moment2, grads)]
    step1 = adam_update(*(a[:, :CUT] for a in arrays))
    step2 = adam_update(*(a[:, CUT:] for a in arrays))
    own1 = jnp.where(moving, rotate(step1, "z", 4), step1)
    own2 = jnp.where(moving, rotate(step2, "z", 4), step2)

    wide = jnp.concatenate(
        [tokens, jnp.pad(routes, ((0, 0), (0, 120))).astype(jnp.bfloat16)], axis=1
    )
    wide = after(wide, step2)
    if Y_WAY == "gather":
        wide = lax.all_gather(wide, "y", axis=0, tiled=False)
    else:
        wide = jnp.broadcast_to(wide[None], (4, *wide.shape))
        wide = lax.all_to_all(wide, "y", split_axis=0, concat_axis=0, tiled=True)
    if TIE_OWN1:
        own1 = after(own1, wide)
    other1 = rotate(own1, "w", 1)
    wide = after(wide, other1)
    named = wide[:, :, width : width + routes.shape[1]].astype(jnp.int32)
    here = expert_of.reshape(8, 4, 2)[:, lax.axis_index("y")].reshape(16)
    outgoing = slot_rows(wide[:, :, :width], named, here)

    first = over_x(own1)
    both = jnp.concatenate([other1, own2], axis=1)
    if SEND == "own1":
        outgoing = after(outgoing, own1)
    elif SEND == "own2":
        outgoing = after(outgoing, own2)
    elif SEND == "first":
        outgoing = after(outgoing, own2, *first[1:])
    elif SEND == "other1":
        outgoing = after(outgoing, own2, other1)
    other2 = rotate(own2, "w", 1)
    if SEND == "x1o1":
        outgoing = after(outgoing, own2, other1, *first[1:])
    elif SEND == "x1o1+":
        outgoing, both, *_ = lax.optimization_barrier((outgoing, both, *first[1:]))
    elif SEND == "x1o1o2":
        outgoing = after(outgoing, own2, other1, other2, *first[1:])
    elif SEND == "o1o2":
        outgoing = after(outgoing, own2, other1, other2)
    arrived = lax.all_to_all(outgoing, ("z", "core"), split_axis=0, concat_axis=0, tiled=True)
    slots = arrived.reshape(owners * CAP, width)

    second = over_x(both)
    third = over_x(other2, *[second[i] for i in FAR_AFTER])

    def hidden_of(blocks):
        blocks = jnp.stack(blocks)
        both = jnp.einsum("xgud,rd->gxur", blocks, slots, preferred_element_type=jnp.float32)
        return (jax.nn.silu(both[0]) * both[1]).astype(jnp.bfloat16)


    def sent_back(own, other):
        own, other = (
            lax.dynamic_slice_in_dim(jnp.concatenate([h, h]), (4 - mine_x) % 4, 4) for h in (own, other)
        )
        every = jnp.where(
            mine_w == 0, jnp.stack([own, other], axis=1), jnp.stack([other, own], axis=1)
        )
        count = every.shape[2]
        every = every.reshape(8, count, owners * CAP)
        back = lax.all_to_all(every, SHARD, split_axis=0, concat_axis=0, tiled=True)
        back = back.reshape(8, count, 8, 2, 4, CAP).transpose(1, 2, 4, 3, 0, 5)
        return back.reshape(count, owners * 8 * CAP)

    hidden_first, hidden_second = hidden_of(first), hidden_of(second)
    if TAIL == 2:
        out1 = sent_back(hidden_first, hidden_second[:, :CUT])
        out2 = sent_back(hidden_second[:, CUT:], hidden_of(third))
        return jnp.concatenate([out1, out2], axis=0)[None]
    own = jnp.concatenate([hidden_first, hidden_second[:, CUT:]], axis=1)
    other = jnp.concatenate([hidden_second[:, :CUT], hidden_of(third)], axis=1)
    return sent_back(own, other)[None]


def solution(mesh):
    grid = Mesh(mesh.devices.reshape(8, 4, 2, 4, 2), EXPERT + SHARD)
    rows = P(EXPERT + SHARD, None)
    units = P(EXPERT, None, SHARD, None)
    return jax.shard_map(
        on_device,
        mesh=grid,
        in_specs=(rows, rows, units, units, units, units, P(), P()),
        out_specs=P(EXPERT, SHARD, None),
        check_vma=False,
    )
```
